32 devices in a mesh: group: 2 (over x), tensor: 4 (over z), rep: 4 (over y, core).
Axes of the slice: x: 2, y: 2, z: 4, core: 2. Of those that a mesh axis runs over, the one named last changes fastest.
Arguments:
- probe_vectors: bfloat16 [128, 64, 128], P(('group', 'rep'), 'tensor'), may hold values from -500 to 500
- stored_lookup_vectors: bfloat16 [128, 8, 512, 128], P(('group', 'rep'), 'tensor'), may hold values from -6 to 6
- stored_content_vectors: bfloat16 [128, 8, 512, 128], P(('group', 'rep'), 'tensor'), may hold values from -6 to 6
- fresh_lookup_vector: bfloat16 [128, 8, 128], P(('group', 'rep'), 'tensor'), may hold values from -6 to 6
- fresh_content_vector: bfloat16 [128, 8, 128], P(('group', 'rep'), 'tensor'), may hold values from -6 to 6
- history_counts: int32 [128], P(('group', 'rep')), may hold values from 1 to 512, as said below
- mixing_matrix: bfloat16 [8192, 8192], P('tensor', ('group', 'rep')), may hold values from -0.25 to 0.25
- skip_stream: bfloat16 [128, 8192], P(('group', 'rep'), 'tensor'), may hold values from -8 to 8
- closing_multiplier: bfloat16 [8192], P('tensor'), may hold values from 0.25 to 1.75
- lexicon_matrix: bfloat16 [8192, 16384], P(None, ('group', 'tensor', 'rep')), may hold values from -0.088388348 to 0.088388348
- sharpening_factor: float32 [128], replicated, may hold values from 0.5 to 20
- desired_perplexity: float32 [128], replicated, may hold values from 6 to 12
- chosen_symbols: int32 [128], replicated, may hold values from 0 to 16383
Outputs:
- hidden: bfloat16 [128, 8192], P(('group', 'rep'), 'tensor')
- next_targets: float32 [128], replicated
- surprise: float32 [128], replicated
The draws below stay inside these ranges and needn't reach their ends.
Inputs may be any that keep to these rules, and one draw needn't show every extreme that they name: `history_counts`: each row holds at least one cached position; some row holds 512.
All inputs are finite; a program needn't handle non-finite values.
Results may differ from the reference program's by a relative error of at most 0.0063.
Values may be sent and summed in bfloat16 or wider, within the bound.
A program may use at most 128 MiB of HBM per device.

```python
import math
import jax
import jax.numpy as jnp
from jax import lax

D = 8192
HEADS = 64
KV_HEADS = 8
HEAD_DIM = 128
CACHE = 512
ROWS = 128
VOCAB = 16384


def shared_rows(key):
    id_key = jax.random.fold_in(key, 11)
    dir_key = jax.random.fold_in(key, 13)
    picked = jax.random.randint(id_key, (ROWS,), 0, VOCAB)
    picked = picked.at[0].set(0).at[ROWS - 1].set(VOCAB - 1)
    direction = jnp.clip(jax.random.normal(dir_key, (ROWS, D), jnp.float32), -3.0, 3.0)
    return (picked, direction)


def draw_probe_vectors(key, part):
    key = jax.random.fold_in(key, 1)
    base = jax.random.normal(key, (ROWS, HEADS, HEAD_DIM), jnp.float32)
    return jnp.clip(base, -500.0, 500.0).astype(jnp.bfloat16)


def draw_history_counts(key, part):
    key = jax.random.fold_in(key, 3)
    picks = jax.random.randint(key, (ROWS,), 1, CACHE + 1)
    history_counts = 1 + (picks * picks - 1) // CACHE
    return history_counts.at[0].set(CACHE).astype(jnp.int32)


def draw_sharpening_factor(key, part):
    key = jax.random.fold_in(key, 5)
    upper = jnp.log(8.0)
    spread = jax.random.uniform(key, (ROWS,), jnp.float32, jnp.log(0.5), upper)
    return jnp.exp(spread).astype(jnp.float32)


def draw_skip_stream(key, part):
    picked, direction = shared_rows(key)
    key = jax.random.fold_in(key, 9)
    fraction = jnp.arange(D, dtype=jnp.float32)[None, :] / D
    row_gain = jax.random.uniform(jax.random.fold_in(key, 2), (ROWS, 1), jnp.float32, 0.7, 1.4)
    base = jax.random.normal(key, (ROWS, D), jnp.float32)
    scale = 0.2 * jnp.exp(fraction * jnp.log(15.0))
    return jnp.clip(base * scale * row_gain + 0.6 * direction, -8.0, 8.0).astype(jnp.bfloat16)


def draw_lexicon_matrix(key, part):
    picked, direction = shared_rows(key)
    key = jax.random.fold_in(key, 17)
    limit = 8.0 * D ** (-0.5)
    base = jax.random.normal(key, (D, VOCAB), jnp.float32) * (2.0 * D ** (-0.5))
    strength = jax.random.uniform(jax.random.fold_in(key, 2), (ROWS,), jnp.float32, 0.22, 0.6)
    columns = direction.T * strength[None, :] * D ** (-0.5)
    lexicon = base.at[:, picked].add(columns)
    return jnp.clip(lexicon, -limit, limit).astype(jnp.bfloat16)


def draw_chosen_symbols(key, part):
    picked, direction = shared_rows(key)
    return picked.astype(jnp.int32)


def level_of(key, shape, split, low, high):
    factor_of = 1.0
    for dim, blocks in split:
        steps = jax.random.uniform(jax.random.fold_in(jax.random.fold_in(key, 6), dim), (blocks,), jnp.float32, low / len(split), high / len(split))
        factor_of = factor_of * jnp.repeat(jnp.exp(steps), shape[dim] // blocks).reshape((-1,) + (1,) * (len(shape) - 1 - dim))
    return factor_of


def bell_draw(key, extent, scale, most, cuts=(), held_as=jnp.bfloat16):
    factor_of = level_of(key, extent, cuts, -0.22, 0.18) if cuts else 1.0
    drawn = jax.random.normal(key, extent, jnp.float32) * scale * factor_of
    return jnp.minimum(jnp.maximum(drawn, -most), most).astype(held_as)


def setup_inputs(seed: int = 0) -> dict:
    seeds = jax.random.split(jax.random.key(seed), 14)
    return {
        "probe_vectors": draw_probe_vectors(jax.random.fold_in(seeds[13], 71), 0),
        "stored_lookup_vectors": bell_draw(seeds[1], (ROWS, KV_HEADS, CACHE, HEAD_DIM), 1.0, 6.0, ((0, 8), (1, 4))),
        "stored_content_vectors": bell_draw(seeds[2], (ROWS, KV_HEADS, CACHE, HEAD_DIM), 1.0, 6.0, ((0, 8), (1, 4))),
        "fresh_lookup_vector": bell_draw(seeds[3], (ROWS, KV_HEADS, HEAD_DIM), 1.0, 6.0, ((0, 8), (1, 4))),
        "fresh_content_vector": bell_draw(seeds[4], (ROWS, KV_HEADS, HEAD_DIM), 1.0, 6.0, ((0, 8), (1, 4))),
        "history_counts": draw_history_counts(jax.random.fold_in(seeds[13], 71), 0),
        "mixing_matrix": bell_draw(seeds[6], (HEADS * HEAD_DIM, D), (HEADS * HEAD_DIM // 16) ** -0.5, 0.25, ((0, 4), (1, 8))),
        "skip_stream": draw_skip_stream(jax.random.fold_in(seeds[13], 71), 0),
        "closing_multiplier": jnp.clip(1.0 + 0.15 * jax.random.normal(seeds[8], (D,), jnp.float32), 0.25, 1.75).astype(jnp.bfloat16),
        "lexicon_matrix": draw_lexicon_matrix(jax.random.fold_in(seeds[13], 71), 0),
        "sharpening_factor": draw_sharpening_factor(jax.random.fold_in(seeds[13], 71), 0),
        "desired_perplexity": jnp.clip(jax.random.uniform(seeds[11], (ROWS,), jnp.float32, 6.0, 12.0), 6.0, 12.0),
        "chosen_symbols": draw_chosen_symbols(jax.random.fold_in(seeds[13], 71), 0),
    }


cut_slope = 4.0

def attend_row(item):
    probe_vectors, keys, values, own_key, own_value, length = item
    group = HEADS // KV_HEADS
    grouped_query_rows = probe_vectors.astype(jnp.float32).reshape(KV_HEADS, group, HEAD_DIM)
    score_scale = 1.0 / math.sqrt(HEAD_DIM)
    scores = jnp.einsum('kgd,kld->kgl', grouped_query_rows, keys.astype(jnp.float32)) * score_scale
    self_entry = jnp.einsum('kgd,kd->kg', grouped_query_rows, own_key.astype(jnp.float32)) * score_scale
    position = jnp.arange(CACHE, dtype=jnp.int32)[None, None, :]
    live = position < length
    top = jnp.maximum(lax.optimization_barrier(jnp.max(jnp.where(live, scores, -1e+30), axis=2)), self_entry)
    expo = jnp.where(live, jnp.exp(scores - top[..., None]), 0.0)
    own_expo = jnp.exp(self_entry - top)
    total = lax.optimization_barrier(jnp.sum(expo, axis=2)) + own_expo
    attention_weights = lax.optimization_barrier(expo.astype(jnp.bfloat16)).astype(jnp.float32)
    self_weight = lax.optimization_barrier(own_expo.astype(jnp.bfloat16)).astype(jnp.float32)
    accum = jnp.einsum('kgl,kld->kgd', attention_weights, values.astype(jnp.float32))
    accum = accum + jnp.einsum('kg,kd->kgd', self_weight, own_value.astype(jnp.float32))
    return (accum / total[..., None]).reshape(HEADS * HEAD_DIM).astype(jnp.bfloat16)

def reference(probe_vectors, stored_lookup_vectors, stored_content_vectors, fresh_lookup_vector, fresh_content_vector, history_counts, mixing_matrix, skip_stream, closing_multiplier, lexicon_matrix, sharpening_factor, desired_perplexity, chosen_symbols):
    attn = lax.map(attend_row, (probe_vectors, stored_lookup_vectors, stored_content_vectors, fresh_lookup_vector, fresh_content_vector, history_counts))
    projected = jnp.dot(attn, mixing_matrix, preferred_element_type=jnp.float32)
    hidden = (skip_stream.astype(jnp.float32) + projected).astype(jnp.bfloat16)
    wide = hidden.astype(jnp.float32)
    mean_sq = lax.optimization_barrier(jnp.mean(wide * wide, axis=1))
    rescaled_stream = (wide * lax.rsqrt(mean_sq + 1e-05)[:, None] * closing_multiplier.astype(jnp.float32)).astype(jnp.bfloat16)
    unnormalized_odds = jnp.dot(rescaled_stream, lexicon_matrix, preferred_element_type=jnp.float32) * sharpening_factor[:, None]
    top = lax.optimization_barrier(jnp.max(unnormalized_odds, axis=1))
    lognorm = top + jnp.log(lax.optimization_barrier(jnp.sum(jnp.exp(unnormalized_odds - top[:, None]), axis=1)))
    logp = unnormalized_odds - lognorm[:, None]
    bits = -logp / math.log(2.0)
    logw = logp + jax.nn.log_sigmoid(cut_slope * (desired_perplexity[:, None] - bits))
    kept = lax.optimization_barrier(jnp.sum(jnp.exp(logw), axis=1))
    hit = jnp.arange(VOCAB, dtype=jnp.int32)[None, :] == chosen_symbols[:, None]
    token_logit = lax.optimization_barrier(jnp.sum(jnp.where(hit, unnormalized_odds, 0.0), axis=1))
    token_logp = token_logit - lognorm
    token_logw = token_logp + jax.nn.log_sigmoid(cut_slope * (desired_perplexity + token_logp / math.log(2.0)))
    surprise = -(token_logw - jnp.log(kept)) / math.log(2.0)
    next_targets = desired_perplexity - 0.1 * (surprise - 5.0)
    return (hidden, next_targets, surprise)
```

```python
import functools
import math

import jax
import jax.numpy as jnp
from jax import lax
from jax.experimental import pallas as pl
from jax.experimental.pallas import tpu as pltpu
from jax.sharding import PartitionSpec as P

cut_slope = 4.0
MESH = pl.DeviceIdType.MESH


def attend(
    probe_vectors,
    stored_lookup_vectors,
    stored_content_vectors,
    fresh_lookup_vector,
    fresh_content_vector,
    history_counts,
):
    rows, kv_local, cache_len, head_dim = stored_lookup_vectors.shape
    heads_local = probe_vectors.shape[1]
    grouped_query_rows = probe_vectors.reshape(rows, kv_local, heads_local // kv_local, head_dim)
    score_scale = 1.0 / math.sqrt(head_dim)
    self_entry = (
        jnp.einsum(
            "mjqo,mjo->mjq",
            grouped_query_rows,
            fresh_lookup_vector,
            preferred_element_type=jnp.float32,
        )
        * score_scale
    )
    scores = (
        jnp.einsum(
            "bkgd,bkld->bkgl",
            grouped_query_rows,
            stored_lookup_vectors,
            preferred_element_type=jnp.float32,
        )
        * score_scale
    )
    position = lax.broadcasted_iota(jnp.int32, (1, 1, 1, cache_len), 3)
    live = position < history_counts[:, None, None, None]
    top = jnp.maximum(jnp.max(jnp.where(live, scores, -1e30), axis=3), self_entry)
    expo = jnp.where(live, jnp.exp(scores - top[..., None]), 0.0)
    total = jnp.sum(expo, axis=3)
    accum = jnp.einsum(
        "bkgl,bkld->bkgd",
        expo.astype(jnp.bfloat16),
        stored_content_vectors,
        preferred_element_type=jnp.float32,
    )
    own_expo = jnp.exp(self_entry - top)
    total = total + own_expo
    accum = accum + jnp.einsum(
        "vct,vcn->vctn",
        own_expo.astype(jnp.bfloat16),
        fresh_content_vector,
        preferred_element_type=jnp.float32,
    )
    return (accum / total[..., None]).reshape(rows, heads_local * head_dim).astype(jnp.bfloat16)


axes = ("group", "tensor", "rep")


def local_wait(ref, sem):
    pltpu.make_async_copy(ref, ref, sem).wait()


def tail_kernel(
    sizes,
    attn_ref,
    mixing_hbm,
    skip_ref,
    gain_ref,
    lexicon_hbm,
    sharp_ref,
    mu_ref,
    chosen_ref,
    hidden_ref,
    targets_ref,
    surprise_ref,
    mixing,
    lexicon,
    every_attn,
    part,
    outgoing,
    incoming,
    skip_block,
    gains,
    state,
    logits,
    squares,
    stats,
    kept_parts,
    load_sems,
    attn_send,
    attn_recv,
    skip_send,
    skip_recv,
    gain_send,
    gain_recv,
    part_send,
    part_recv,
    column_send,
    plane_send,
    pair_send,
    state_recv,
    stats_sems,
    kept_sems,
):
    G, T, R = sizes
    N = G * T * R
    columns = G * R
    fold = columns // T
    pairs = R // 2
    own_rows = attn_ref.shape[0]
    rows = every_attn.shape[0]
    block_rows = rows // T
    width = mixing.shape[1]
    vocab_local = lexicon.shape[1]

    g, t, r = (lax.axis_index(a) for a in axes)
    pair, core = r // 2, r % 2
    other = 1 - core
    column = g * R + r
    twin = g * R + pair * 2 + other
    me = (g * T + t) * R + r

    load_mixing = pltpu.make_async_copy(mixing_hbm, mixing, load_sems.at[0])
    load_lexicon = pltpu.make_async_copy(lexicon_hbm, lexicon, load_sems.at[1])
    load_mixing.start()
    load_lexicon.start()

    def device_of(index):
        return (index // (T * R), (index // R) % T, index % R)

    barrier = pltpu.get_barrier_semaphore()

    @pl.loop(1, N)
    def _(step):
        pl.semaphore_signal(
            barrier, inc=1, device_id=device_of((me + step) % N), device_id_type=MESH
        )

    pl.semaphore_wait(barrier, N - 1)

    def push(src, dst, send_sem, recv_sem, device):
        copy = pltpu.make_async_remote_copy(
            src_ref=src,
            dst_ref=dst,
            send_sem=send_sem,
            recv_sem=recv_sem,
            device_id=device,
            device_id_type=MESH,
        )
        copy.start()
        return copy

    peers = [(a, b) for a in range(G) for b in range(pairs) if (a, b) != (0, 0)]

    def peer_to(a, b):
        return (g + a) % G, ((pair + b) % pairs) * 2 + core

    def peer_from(a, b):
        return ((g + G - a) % G) * R + ((pair + pairs - b) % pairs) * 2

    sibling = (g, t, pair * 2 + other)

    def attn_rows(index):
        return every_attn.at[pl.ds(pl.multiple_of(index * own_rows, own_rows), own_rows), :]

    sends = []
    for n, (a, b) in enumerate(peers):
        to_g, to_r = peer_to(a, b)
        sends.append(
            push(attn_ref, attn_rows(column), attn_send.at[n], attn_recv.at[column], (to_g, t, to_r))
        )
    sends.append(
        push(attn_ref, attn_rows(column), attn_send.at[len(peers)], attn_recv.at[column], sibling)
    )
    every_attn[pl.ds(pl.multiple_of(column * own_rows, own_rows), own_rows), :] = attn_ref[...]

    home_t = column // fold
    home_slot = column % fold

    def skip_rows(slot):
        return skip_block.at[pl.ds(pl.multiple_of(slot * own_rows, own_rows), own_rows), :]

    for j in range(fold):
        dest = t * fold + j
        away = jnp.logical_or(dest != column, home_t != t)
        source = skip_ref.at[:, pl.ds(j * width, width)]

        @pl.when(away)
        def _():
            push(
                source,
                skip_rows(home_slot),
                skip_send.at[j],
                skip_recv.at[home_slot],
                (dest // R, home_t, dest % R),
            )

        @pl.when(jnp.logical_not(away))
        def _():
            pltpu.make_async_copy(source, skip_rows(home_slot), skip_recv.at[home_slot]).start()

    gains[pl.ds(t * fold, fold)] = gain_ref[...]
    for j in range(1, T):
        sends.append(
            push(
                gain_ref,
                gains.at[pl.ds(t * fold, fold)],
                gain_send.at[j],
                gain_recv.at[t],
                (g, (t + j) % T, r),
            )
        )

    for n, (a, b) in enumerate(peers):
        source = peer_from(a, b) + core
        local_wait(attn_rows(source), attn_recv.at[source])
        sends.append(
            push(
                attn_rows(source),
                attn_rows(source),
                attn_send.at[len(peers) + 1 + n],
                attn_recv.at[source],
                sibling,
            )
        )
    local_wait(attn_rows(twin), attn_recv.at[twin])
    for a, b in peers:
        source = peer_from(a, b) + other
        local_wait(attn_rows(source), attn_recv.at[source])

    load_mixing.wait()
    tile = min(256, width)

    @pl.loop(0, width // tile)
    def _(index):
        span = pl.ds(pl.multiple_of(index * tile, tile), tile)
        product = jnp.dot(every_attn[...], mixing[:, span], preferred_element_type=jnp.float32)
        part[:, span] = product
        outgoing[:, span] = product.astype(jnp.bfloat16)

    def block_of(index):
        return pl.ds(pl.multiple_of(index * block_rows, block_rows), block_rows)

    for j in range(1, T):
        to_t = (t + j) % T
        sends.append(
            push(
                outgoing.at[block_of(to_t), :],
                incoming.at[t],
                part_send.at[j],
                part_recv.at[t],
                (g, to_t, r),
            )
        )
    for j in range(fold):
        local_wait(skip_rows(j), skip_recv.at[j])
    total = part[block_of(t), :]
    for j in range(1, T):
        from_t = (t + j) % T
        local_wait(incoming.at[from_t], part_recv.at[from_t])
        total = total + incoming[from_t].astype(jnp.float32)
    hidden = (skip_block[...].astype(jnp.float32) + total).astype(jnp.bfloat16)
    state[column, block_of(t), :] = hidden

    def state_block(col, index):
        return state.at[col, block_of(index), :]

    def spread(index):
        for a, b in peers:
            to_g, to_r = peer_to(a, b)
            push(
                state_block(column, index),
                state_block(column, index),
                plane_send,
                state_recv.at[column, index],
                (to_g, t, to_r),
            )
        push(
            state_block(column, index),
            state_block(column, index),
            plane_send,
            state_recv.at[column, index],
            sibling,
        )

    for j in range(1, T):
        push(
            state_block(column, t),
            state_block(column, t),
            column_send,
            state_recv.at[column, t],
            (g, (t + j) % T, r),
        )
    spread(t)
    for j in range(1, T):
        from_t = (t + j) % T
        local_wait(gains.at[pl.ds(from_t * fold, fold)], gain_recv.at[from_t])
    load_lexicon.wait()
    logits[...] = jnp.zeros_like(logits)
    squares[...] = jnp.zeros_like(squares)

    def head(col):
        wide = state[col].astype(jnp.float32)
        squared = wide * wide
        summed = squares[...]
        for n in range(width // 128):
            summed = summed + squared[:, n * 128 : (n + 1) * 128]
        squares[...] = summed
        scaled = (wide * gains[col]).astype(jnp.bfloat16)
        block = lexicon[pl.ds(pl.multiple_of(col * width, width), width), :]
        logits[...] += jnp.dot(scaled, block, preferred_element_type=jnp.float32)

    for j in range(1, T):
        from_t = (t + j) % T
        local_wait(state_block(column, from_t), state_recv.at[column, from_t])
        spread(from_t)
    head(column)
    for j in range(T):
        from_t = (t + j) % T
        local_wait(state_block(twin, from_t), state_recv.at[twin, from_t])
    head(twin)

    @pl.loop(1, G * pairs)
    def _(step):
        source = peer_from(step // pairs, step % pairs)
        for j in range(T):
            from_t = (t + j) % T
            block = state_block(source + core, from_t)
            local_wait(block, state_recv.at[source + core, from_t])
            push(block, block, pair_send, state_recv.at[source + core, from_t], sibling)
        head(source + core)
        for j in range(T):
            from_t = (t + j) % T
            local_wait(
                state_block(source + other, from_t), state_recv.at[source + other, from_t]
            )
        head(source + other)

    own_span = pl.ds(pl.multiple_of(column * own_rows, own_rows), own_rows)
    for j in range(fold):
        hidden_ref[:, j * width : (j + 1) * width] = state[t * fold + j, own_span, :]

    features = columns * width
    mean_square = jnp.sum(squares[...].T, axis=0, keepdims=True) / features
    row_scale = lax.rsqrt(mean_square + 1e-05) * sharp_ref[...]
    odds = logits[...].T * row_scale
    entry = me * vocab_local + lax.broadcasted_iota(jnp.int32, odds.shape, 0)
    token_part = jnp.sum(jnp.where(entry == chosen_ref[...], odds, 0.0), axis=0, keepdims=True)
    local_top = jnp.max(odds, axis=0, keepdims=True)
    local_total = jnp.sum(jnp.exp(odds - local_top), axis=0, keepdims=True)
    stats[me] = jnp.concatenate(
        [local_top, local_total, token_part, jnp.zeros((5, rows), jnp.float32)], axis=0
    )

    def share(buffer, sems):
        @pl.loop(1, N)
        def _(step):
            push(
                buffer.at[me],
                buffer.at[me],
                sems.at[0],
                sems.at[1],
                device_of((me + step) % N),
            )

        local_wait(buffer.at[pl.ds(0, N - 1)], sems.at[1])

    share(stats, stats_sems)
    tops = stats[:, 0, :]
    top = jnp.max(tops, axis=0, keepdims=True)
    sum_exp = jnp.sum(stats[:, 1, :] * jnp.exp(tops - top), axis=0, keepdims=True)
    token_logit = jnp.sum(stats[:, 2, :], axis=0, keepdims=True)
    lognorm = top + jnp.log(sum_exp)
    mu = mu_ref[...]
    logp = odds - lognorm
    margin = cut_slope * (mu + logp / math.log(2.0))
    tail = jnp.exp(-jnp.abs(margin))
    weight = jnp.where(margin >= 0.0, 1.0, tail) / (1.0 + tail)
    kept_local = jnp.sum(jnp.exp(logp) * weight, axis=0, keepdims=True)
    kept_parts[me] = jnp.broadcast_to(kept_local, (8, rows))
    share(kept_parts, kept_sems)
    kept = jnp.sum(kept_parts[:, 0, :], axis=0, keepdims=True)
    token_logp = token_logit - lognorm
    token_margin = cut_slope * (mu + token_logp / math.log(2.0))
    token_logw = (
        token_logp
        + jnp.minimum(token_margin, 0.0)
        - jnp.log1p(jnp.exp(-jnp.abs(token_margin)))
    )
    surprise = -(token_logw - jnp.log(kept)) / math.log(2.0)
    surprise_ref[...] = surprise
    targets_ref[...] = mu - 0.1 * (surprise - 5.0)

    for copy in sends:
        copy.wait_send()
    for j in range(fold):
        away = jnp.logical_or(t * fold + j != column, home_t != t)

        @pl.when(away)
        def _():
            local_wait(skip_ref.at[:, pl.ds(j * width, width)], skip_send.at[j])

    local_wait(state.at[0, pl.ds(0, (T - 1) * block_rows), :], column_send)
    local_wait(state.at[pl.ds(0, len(peers) + 1)], plane_send)
    local_wait(state.at[pl.ds(0, len(peers))], pair_send)
    local_wait(stats.at[pl.ds(0, N - 1)], stats_sems.at[0])
    local_wait(kept_parts.at[pl.ds(0, N - 1)], kept_sems.at[0])


def tail(sizes, attn, mixing, skip, gain, lexicon, sharp, mu, chosen):
    G, T, R = sizes
    N = G * T * R
    columns = G * R
    fold = columns // T
    own_rows = attn.shape[0]
    rows = own_rows * columns
    block_rows = rows // T
    width = mixing.shape[1]
    depth = mixing.shape[0]
    features, vocab_local = lexicon.shape
    peers = columns // 2 - 1
    vmem = pl.BlockSpec(memory_space=pltpu.VMEM)
    hbm = pl.BlockSpec(memory_space=pl.ANY)
    dma = pltpu.SemaphoreType.DMA
    hidden, targets, surprise = pl.pallas_call(
        functools.partial(tail_kernel, sizes),
        out_shape=(
            jax.ShapeDtypeStruct(skip.shape, jnp.bfloat16),
            jax.ShapeDtypeStruct((1, rows), jnp.float32),
            jax.ShapeDtypeStruct((1, rows), jnp.float32),
        ),
        in_specs=[vmem, hbm, vmem, vmem, hbm, vmem, vmem, vmem],
        out_specs=(vmem, vmem, vmem),
        scratch_shapes=[
            pltpu.VMEM(mixing.shape, jnp.bfloat16),
            pltpu.VMEM(lexicon.shape, jnp.bfloat16),
            pltpu.VMEM((rows, depth), jnp.bfloat16),
            pltpu.VMEM((rows, width), jnp.float32),
            pltpu.VMEM((rows, width), jnp.bfloat16),
            pltpu.VMEM((T, block_rows, width), jnp.bfloat16),
            pltpu.VMEM((block_rows, width), jnp.bfloat16),
            pltpu.VMEM((columns, 1, width), jnp.float32),
            pltpu.VMEM((columns, rows, width), jnp.bfloat16),
            pltpu.VMEM((rows, vocab_local), jnp.float32),
            pltpu.VMEM((rows, 128), jnp.float32),
            pltpu.VMEM((N, 8, rows), jnp.float32),
            pltpu.VMEM((N, 8, rows), jnp.float32),
            dma((2,)),
            dma((2 * peers + 1,)),
            dma((columns,)),
            dma((fold,)),
            dma((fold,)),
            dma((T,)),
            dma((T,)),
            dma((T,)),
            dma((T,)),
            dma,
            dma,
            dma,
            dma((columns, T)),
            dma((2,)),
            dma((2,)),
        ],
        compiler_params=pltpu.CompilerParams(
            collective_id=0, has_side_effects=True, vmem_limit_bytes=56 * 2**20
        ),
    )(
        attn,
        mixing,
        skip,
        gain.astype(jnp.float32).reshape(fold, 1, width),
        lexicon,
        sharp.reshape(1, rows),
        mu.reshape(1, rows),
        chosen.reshape(1, rows),
    )
    return hidden, targets.reshape(rows), surprise.reshape(rows)


def solution(mesh):
    sizes = tuple(mesh.shape[a] for a in axes)

    def shards(
        probe_vectors,
        stored_lookup_vectors,
        stored_content_vectors,
        fresh_lookup_vector,
        fresh_content_vector,
        history_counts,
        mixing_matrix,
        skip_stream,
        closing_multiplier,
        lexicon_matrix,
        sharpening_factor,
        desired_perplexity,
        chosen_symbols,
    ):
        attn = attend(
            probe_vectors,
            stored_lookup_vectors,
            stored_content_vectors,
            fresh_lookup_vector,
            fresh_content_vector,
            history_counts,
        )
        return tail(
            sizes,
            attn,
            mixing_matrix,
            skip_stream,
            closing_multiplier,
            lexicon_matrix,
            sharpening_factor,
            desired_perplexity,
            chosen_symbols,
        )

    placed = (
        P(("group", "rep"), "tensor", None),
        P(("group", "rep"), "tensor", None, None),
        P(("group", "rep"), "tensor", None, None),
        P(("group", "rep"), "tensor", None),
        P(("group", "rep"), "tensor", None),
        P(("group", "rep")),
        P("tensor", ("group", "rep")),
        P(("group", "rep"), "tensor"),
        P("tensor"),
        P(None, ("group", "tensor", "rep")),
        P(),
        P(),
        P(),
    )
    return jax.shard_map(
        shards,
        mesh=mesh,
        in_specs=placed,
        out_specs=(P(("group", "rep"), "tensor"), P(), P()),
        check_vma=False,
    )
```

```python
import functools
import math

import jax
import jax.numpy as jnp
from jax import lax
from jax.experimental import pallas as pl
from jax.experimental.pallas import tpu as pltpu
from jax.sharding import PartitionSpec as P

cut_slope = 4.0
MESH = pl.DeviceIdType.MESH


axes = ("group", "tensor", "rep")


def local_wait(ref, sem):
    pltpu.make_async_copy(ref, ref, sem).wait()


def tail_kernel(
    sizes,
    probe_ref,
    keys_hbm,
    values_hbm,
    own_key_ref,
    own_value_ref,
    counts_ref,
    mixing_hbm,
    skip_ref,
    gain_ref,
    lexicon_hbm,
    sharp_ref,
    mu_ref,
    chosen_ref,
    hidden_ref,
    targets_ref,
    surprise_ref,
    keys,
    values,
    row_attn,
    attn_ref,
    mixing,
    lexicon,
    every_attn,
    part,
    incoming,
    skip_block,
    gain_block,
    hidden_block,
    square_sums,
    state,
    logits,
    stats,
    kept_parts,
    cache_sems,
    load_sems,
    attn_send,
    attn_recv,
    skip_send,
    skip_recv,
    gain_send,
    gain_recv,
    back_send,
    back_recv,
    square_sems,
    part_send,
    part_recv,
    column_send,
    plane_send,
    pair_send,
    state_recv,
    stats_sems,
    kept_sems,
):
    G, T, R = sizes
    N = G * T * R
    columns = G * R
    fold = columns // T
    pairs = R // 2
    own_rows, heads, head_dim = probe_ref.shape
    kv_heads = own_key_ref.shape[1]
    cache_len = keys.shape[2]
    rows = every_attn.shape[0]
    block_rows = rows // T
    width = mixing.shape[1]
    vocab_local = lexicon.shape[1]

    g, t, r = (lax.axis_index(a) for a in axes)
    pair, core = r // 2, r % 2
    other = 1 - core
    column = g * R + r
    twin = g * R + pair * 2 + other
    me = (g * T + t) * R + r

    load_mixing = pltpu.make_async_copy(mixing_hbm, mixing, load_sems.at[0])
    load_lexicon = pltpu.make_async_copy(lexicon_hbm, lexicon, load_sems.at[1])
    group_rows = own_rows // cache_sems.shape[1]

    def cache_loads(index):
        span = pl.ds(index * group_rows, group_rows)
        return [
            pltpu.make_async_copy(source.at[span], dest.at[span], cache_sems.at[n, index])
            for n, (source, dest) in enumerate(((keys_hbm, keys), (values_hbm, values)))
        ]

    @pl.loop(0, own_rows // group_rows)
    def _(index):
        for load in cache_loads(index):
            load.start()

    load_mixing.start()
    load_lexicon.start()

    def wrap(position, size):
        return jnp.where(position >= size, position - size, position)

    def every_other(visit):
        for a in range(G):
            to_g = wrap(g + a, G)

            @pl.loop(1 if a == 0 else 0, T)
            def _(b):
                to_t = wrap(t + b, T)
                for d in range(R):
                    visit((to_g, to_t, wrap(r + d, R)))

        for d in range(1, R):
            visit((g, t, wrap(r + d, R)))

    barrier = pltpu.get_barrier_semaphore()
    every_other(
        lambda device: pl.semaphore_signal(
            barrier, inc=1, device_id=device, device_id_type=MESH
        )
    )

    score_scale = 1.0 / math.sqrt(head_dim)
    share_of = heads // kv_heads
    position = lax.broadcasted_iota(jnp.int32, (heads, cache_len), 1)

    def spread_heads(pair_rows):
        wide = pair_rows.astype(jnp.float32)
        return jnp.concatenate(
            [jnp.broadcast_to(wide[k : k + 1], (share_of, head_dim)) for k in range(kv_heads)],
            axis=0,
        )

    def per_head(products):
        return jnp.concatenate(
            [products[k][k * share_of : (k + 1) * share_of] for k in range(kv_heads)], axis=0
        )

    def attend(row):
        query = probe_ref[row]
        scores = score_scale * per_head(
            [
                lax.dot_general(
                    query,
                    keys[row, k],
                    (((1,), (1,)), ((), ())),
                    preferred_element_type=jnp.float32,
                )
                for k in range(kv_heads)
            ]
        )
        own = score_scale * jnp.sum(
            query.astype(jnp.float32) * spread_heads(own_key_ref[row]), axis=1, keepdims=True
        )
        live = position < counts_ref[row]
        peak = jnp.maximum(
            jnp.max(jnp.where(live, scores, -1e30), axis=1, keepdims=True), own
        )
        expo = jnp.where(live, jnp.exp(scores - peak), 0.0)
        own_expo = jnp.exp(own - peak)
        total = jnp.sum(expo, axis=1, keepdims=True) + own_expo
        weights = expo.astype(jnp.bfloat16)
        accum = per_head(
            [
                jnp.dot(weights, values[row, k], preferred_element_type=jnp.float32)
                for k in range(kv_heads)
            ]
        )
        own_weight = own_expo.astype(jnp.bfloat16).astype(jnp.float32)
        accum = accum + own_weight * spread_heads(own_value_ref[row])
        row_attn[row] = accum / total

    @pl.loop(0, own_rows // group_rows)
    def _(index):
        for load in cache_loads(index):
            load.wait()
        for n in range(group_rows):
            attend(index * group_rows + n)

    for h in range(heads):
        attn_ref[:, h * head_dim : (h + 1) * head_dim] = row_attn[:, h, :].astype(jnp.bfloat16)

    pl.semaphore_wait(barrier, N - 1)

    def push(src, dst, send_sem, recv_sem, device):
        copy = pltpu.make_async_remote_copy(
            src_ref=src,
            dst_ref=dst,
            send_sem=send_sem,
            recv_sem=recv_sem,
            device_id=device,
            device_id_type=MESH,
        )
        copy.start()
        return copy

    peers = [(a, b) for a in range(G) for b in range(pairs) if (a, b) != (0, 0)]

    def peer_to(a, b):
        return (g + a) % G, ((pair + b) % pairs) * 2 + core

    def peer_from(a, b):
        return ((g + G - a) % G) * R + ((pair + pairs - b) % pairs) * 2

    sibling = (g, t, pair * 2 + other)

    def attn_rows(index):
        return every_attn.at[pl.ds(pl.multiple_of(index * own_rows, own_rows), own_rows), :]

    sends = []
    for n, (a, b) in enumerate(peers):
        to_g, to_r = peer_to(a, b)
        sends.append(
            push(attn_ref, attn_rows(column), attn_send.at[n], attn_recv.at[column], (to_g, t, to_r))
        )
    sends.append(
        push(attn_ref, attn_rows(column), attn_send.at[len(peers)], attn_recv.at[column], sibling)
    )
    every_attn[pl.ds(pl.multiple_of(column * own_rows, own_rows), own_rows), :] = attn_ref[...]

    home_t = column // fold
    home_slot = column % fold

    def skip_rows(slot):
        return skip_block.at[pl.ds(pl.multiple_of(slot * own_rows, own_rows), own_rows), :]

    for j in range(fold):
        dest = t * fold + j
        away = jnp.logical_or(dest != column, home_t != t)
        source = skip_ref.at[:, pl.ds(j * width, width)]

        @pl.when(away)
        def _():
            push(
                source,
                skip_rows(home_slot),
                skip_send.at[j],
                skip_recv.at[home_slot],
                (dest // R, home_t, dest % R),
            )
            push(
                gain_ref.at[j],
                gain_block.at[home_slot],
                gain_send.at[j],
                gain_recv.at[home_slot],
                (dest // R, home_t, dest % R),
            )

        @pl.when(jnp.logical_not(away))
        def _():
            pltpu.make_async_copy(source, skip_rows(home_slot), skip_recv.at[home_slot]).start()
            pltpu.make_async_copy(
                gain_ref.at[j], gain_block.at[home_slot], gain_recv.at[home_slot]
            ).start()

    for n, (a, b) in enumerate(peers):
        source = peer_from(a, b) + core
        local_wait(attn_rows(source), attn_recv.at[source])
        sends.append(
            push(
                attn_rows(source),
                attn_rows(source),
                attn_send.at[len(peers) + 1 + n],
                attn_recv.at[source],
                sibling,
            )
        )
    local_wait(attn_rows(twin), attn_recv.at[twin])
    for a, b in peers:
        source = peer_from(a, b) + other
        local_wait(attn_rows(source), attn_recv.at[source])

    load_mixing.wait()
    tile = min(256, width)

    @pl.loop(0, width // tile)
    def _(index):
        span = pl.ds(pl.multiple_of(index * tile, tile), tile)
        part[:, span] = jnp.dot(
            every_attn[...], mixing[:, span], preferred_element_type=jnp.float32
        )

    def block_of(index):
        return pl.ds(pl.multiple_of(index * block_rows, block_rows), block_rows)

    for j in range(1, T):
        to_t = (t + j) % T
        sends.append(
            push(
                part.at[block_of(to_t), :],
                incoming.at[t],
                part_send.at[j],
                part_recv.at[t],
                (g, to_t, r),
            )
        )
    for j in range(fold):
        local_wait(skip_rows(j), skip_recv.at[j])
        local_wait(gain_block.at[j], gain_recv.at[j])
    total = part[block_of(t), :]
    for j in range(1, T):
        from_t = (t + j) % T
        local_wait(incoming.at[from_t], part_recv.at[from_t])
        total = total + incoming[from_t]
    hidden = (skip_block[...].astype(jnp.float32) + total).astype(jnp.bfloat16)
    hidden_block[...] = hidden

    def back_target(j):
        owner = t * fold + j
        return owner, column // fold, column % fold

    def hidden_slot(slot):
        return hidden_ref.at[:, pl.ds(pl.multiple_of(slot * width, width), width)]

    wide = hidden.astype(jnp.float32)
    row_squares = jnp.sum(wide * wide, axis=1, keepdims=True)
    diagonal = lax.broadcasted_iota(jnp.int32, (block_rows, 128), 1) == (
        lax.broadcasted_iota(jnp.int32, (block_rows, 128), 0)
    )
    square_sums[column] = jnp.sum(
        jnp.where(diagonal, row_squares, 0.0), axis=0, keepdims=True
    )
    for a in range(G):
        for d in range(R):
            if (a, d) != (0, 0):
                push(
                    square_sums.at[column],
                    square_sums.at[column],
                    square_sems.at[0],
                    square_sems.at[1],
                    (wrap(g + a, G), t, wrap(r + d, R)),
                )
    for j in range(fold):
        owner, at_t, slot = back_target(j)
        away = jnp.logical_or(owner != column, at_t != t)
        source = hidden_block.at[pl.ds(j * own_rows, own_rows), :]

        @pl.when(away)
        def _():
            push(
                source,
                hidden_slot(slot),
                back_send.at[j],
                back_recv.at[slot],
                (owner // R, at_t, owner % R),
            )

        @pl.when(jnp.logical_not(away))
        def _():
            pltpu.make_async_copy(source, hidden_slot(slot), back_recv.at[slot]).start()

    local_wait(square_sums.at[pl.ds(0, columns - 1)], square_sems.at[1])
    mean_square = jnp.sum(square_sums[...], axis=0) / (columns * width)
    scale = lax.rsqrt(
        jnp.sum(jnp.where(diagonal, mean_square, 0.0), axis=1, keepdims=True) + 1e-05
    )
    state[column, block_of(t), :] = (wide * scale * gain_block[0]).astype(jnp.bfloat16)

    def state_block(col, index):
        return state.at[col, block_of(index), :]

    def spread(index):
        for a, b in peers:
            to_g, to_r = peer_to(a, b)
            push(
                state_block(column, index),
                state_block(column, index),
                plane_send,
                state_recv.at[column, index],
                (to_g, t, to_r),
            )
        push(
            state_block(column, index),
            state_block(column, index),
            plane_send,
            state_recv.at[column, index],
            sibling,
        )

    for j in range(1, T):
        push(
            state_block(column, t),
            state_block(column, t),
            column_send,
            state_recv.at[column, t],
            (g, (t + j) % T, r),
        )
    spread(t)
    load_lexicon.wait()
    logits[...] = jnp.zeros_like(logits)

    def head(col):
        block = lexicon[pl.ds(pl.multiple_of(col * width, width), width), :]
        logits[...] += jnp.dot(state[col], block, preferred_element_type=jnp.float32)

    for j in range(1, T):
        from_t = (t + j) % T
        local_wait(state_block(column, from_t), state_recv.at[column, from_t])
        spread(from_t)
    head(column)
    for j in range(T):
        from_t = (t + j) % T
        local_wait(state_block(twin, from_t), state_recv.at[twin, from_t])
    head(twin)

    @pl.loop(1, G * pairs)
    def _(step):
        source = peer_from(step // pairs, step % pairs)
        for j in range(T):
            from_t = (t + j) % T
            block = state_block(source + core, from_t)
            local_wait(block, state_recv.at[source + core, from_t])
            push(block, block, pair_send, state_recv.at[source + core, from_t], sibling)
        head(source + core)
        for j in range(T):
            from_t = (t + j) % T
            local_wait(
                state_block(source + other, from_t), state_recv.at[source + other, from_t]
            )
        head(source + other)

    odds = logits[...].T * sharp_ref[...]
    entry = me * vocab_local + lax.broadcasted_iota(jnp.int32, odds.shape, 0)
    token_part = jnp.sum(jnp.where(entry == chosen_ref[...], odds, 0.0), axis=0, keepdims=True)
    local_top = jnp.max(odds, axis=0, keepdims=True)
    local_total = jnp.sum(jnp.exp(odds - local_top), axis=0, keepdims=True)
    stats[me] = jnp.concatenate(
        [local_top, local_total, token_part, jnp.zeros((5, rows), jnp.float32)], axis=0
    )

    def share(buffer, sems):
        every_other(
            lambda device: push(
                buffer.at[me], buffer.at[me], sems.at[0], sems.at[1], device
            )
        )
        local_wait(buffer.at[pl.ds(0, N - 1)], sems.at[1])

    share(stats, stats_sems)
    tops = stats[:, 0, :]
    top = jnp.max(tops, axis=0, keepdims=True)
    sum_exp = jnp.sum(stats[:, 1, :] * jnp.exp(tops - top), axis=0, keepdims=True)
    token_logit = jnp.sum(stats[:, 2, :], axis=0, keepdims=True)
    lognorm = top + jnp.log(sum_exp)
    mu = mu_ref[...]
    logp = odds - lognorm
    margin = cut_slope * (mu + logp / math.log(2.0))
    tail = jnp.exp(-jnp.abs(margin))
    weight = jnp.where(margin >= 0.0, 1.0, tail) / (1.0 + tail)
    kept_local = jnp.sum(jnp.exp(logp) * weight, axis=0, keepdims=True)
    kept_parts[me] = kept_local
    share(kept_parts, kept_sems)
    kept = jnp.sum(kept_parts[...], axis=0)
    token_logp = token_logit - lognorm
    token_margin = cut_slope * (mu + token_logp / math.log(2.0))
    token_logw = (
        token_logp
        + jnp.minimum(token_margin, 0.0)
        - jnp.log1p(jnp.exp(-jnp.abs(token_margin)))
    )
    surprise = -(token_logw - jnp.log(kept)) / math.log(2.0)
    surprise_ref[...] = surprise
    targets_ref[...] = mu - 0.1 * (surprise - 5.0)

    for copy in sends:
        copy.wait_send()
    for j in range(fold):
        away = jnp.logical_or(t * fold + j != column, home_t != t)

        @pl.when(away)
        def _():
            local_wait(skip_ref.at[:, pl.ds(j * width, width)], skip_send.at[j])
            local_wait(gain_ref.at[j], gain_send.at[j])

        owner, at_t, slot = back_target(j)

        @pl.when(jnp.logical_or(owner != column, at_t != t))
        def _():
            local_wait(hidden_block.at[pl.ds(j * own_rows, own_rows), :], back_send.at[j])

        local_wait(hidden_slot(j), back_recv.at[j])

    local_wait(square_sums.at[pl.ds(0, columns - 1)], square_sems.at[0])
    local_wait(state.at[0, pl.ds(0, (T - 1) * block_rows), :], column_send)
    local_wait(state.at[pl.ds(0, len(peers) + 1)], plane_send)
    local_wait(state.at[pl.ds(0, len(peers))], pair_send)
    local_wait(stats.at[pl.ds(0, N - 1)], stats_sems.at[0])
    local_wait(kept_parts.at[pl.ds(0, N - 1)], kept_sems.at[0])


def finish_kernel(hidden_in, targets_in, surprise_in, hidden_ref, targets_ref, surprise_ref):
    hidden_ref[...] = hidden_in[...]
    targets_ref[...] = targets_in[...]
    surprise_ref[...] = surprise_in[...]


def tail(sizes, probe, keys, values, own_key, own_value, counts, mixing, skip, gain, lexicon, sharp, mu, chosen):
    G, T, R = sizes
    N = G * T * R
    columns = G * R
    fold = columns // T
    own_rows, heads, head_dim = probe.shape
    load_groups = math.gcd(own_rows, 4)
    rows = own_rows * columns
    block_rows = rows // T
    width = mixing.shape[1]
    depth = mixing.shape[0]
    features, vocab_local = lexicon.shape
    peers = columns // 2 - 1
    vmem = pl.BlockSpec(memory_space=pltpu.VMEM)
    hbm = pl.BlockSpec(memory_space=pl.ANY)
    dma = pltpu.SemaphoreType.DMA
    out_shape = (
        jax.ShapeDtypeStruct(skip.shape, jnp.bfloat16),
        jax.ShapeDtypeStruct((1, rows), jnp.float32),
        jax.ShapeDtypeStruct((1, rows), jnp.float32),
    )
    results = pl.pallas_call(
        functools.partial(tail_kernel, sizes),
        out_shape=out_shape,
        in_specs=[vmem, hbm, hbm, vmem, vmem, pl.BlockSpec(memory_space=pltpu.SMEM), hbm, vmem, vmem, hbm, vmem, vmem, vmem],
        out_specs=(vmem, vmem, vmem),
        scratch_shapes=[
            pltpu.VMEM(keys.shape, jnp.bfloat16),
            pltpu.VMEM(values.shape, jnp.bfloat16),
            pltpu.VMEM((own_rows, heads, head_dim), jnp.float32),
            pltpu.VMEM((own_rows, depth), jnp.bfloat16),
            pltpu.VMEM(mixing.shape, jnp.bfloat16),
            pltpu.VMEM(lexicon.shape, jnp.bfloat16),
            pltpu.VMEM((rows, depth), jnp.bfloat16),
            pltpu.VMEM((rows, width), jnp.float32),
            pltpu.VMEM((T, block_rows, width), jnp.float32),
            pltpu.VMEM((block_rows, width), jnp.bfloat16),
            pltpu.VMEM((fold, 1, width), jnp.float32),
            pltpu.VMEM((block_rows, width), jnp.bfloat16),
            pltpu.VMEM((columns, 1, 128), jnp.float32),
            pltpu.VMEM((columns, rows, width), jnp.bfloat16),
            pltpu.VMEM((rows, vocab_local), jnp.float32),
            pltpu.VMEM((N, 8, rows), jnp.float32),
            pltpu.VMEM((N, 1, rows), jnp.float32),
            dma((2, load_groups)),
            dma((2,)),
            dma((2 * peers + 1,)),
            dma((columns,)),
            dma((fold,)),
            dma((fold,)),
            dma((fold,)),
            dma((fold,)),
            dma((fold,)),
            dma((fold,)),
            dma((2,)),
            dma((T,)),
            dma((T,)),
            dma,
            dma,
            dma,
            dma((columns, T)),
            dma((2,)),
            dma((2,)),
        ],
        compiler_params=pltpu.CompilerParams(
            collective_id=0, has_side_effects=True, vmem_limit_bytes=56 * 2**20
        ),
    )(
        probe,
        keys,
        values,
        own_key,
        own_value,
        counts,
        mixing,
        skip,
        gain.astype(jnp.float32).reshape(fold, 1, width),
        lexicon,
        sharp.reshape(1, rows),
        mu.reshape(1, rows),
        chosen.reshape(1, rows),
    )
    hidden, targets, surprise = pl.pallas_call(
        finish_kernel, out_shape=out_shape, in_specs=[vmem] * 3, out_specs=(vmem,) * 3
    )(*results)
    return hidden, targets.reshape(rows), surprise.reshape(rows)


def solution(mesh):
    sizes = tuple(mesh.shape[a] for a in axes)

    def shards(
        probe_vectors,
        stored_lookup_vectors,
        stored_content_vectors,
        fresh_lookup_vector,
        fresh_content_vector,
        history_counts,
        mixing_matrix,
        skip_stream,
        closing_multiplier,
        lexicon_matrix,
        sharpening_factor,
        desired_perplexity,
        chosen_symbols,
    ):
        return tail(
            sizes,
            probe_vectors,
            stored_lookup_vectors,
            stored_content_vectors,
            fresh_lookup_vector,
            fresh_content_vector,
            history_counts,
            mixing_matrix,
            skip_stream,
            closing_multiplier,
            lexicon_matrix,
            sharpening_factor,
            desired_perplexity,
            chosen_symbols,
        )

    placed = (
        P(("group", "rep"), "tensor", None),
        P(("group", "rep"), "tensor", None, None),
        P(("group", "rep"), "tensor", None, None),
        P(("group", "rep"), "tensor", None),
        P(("group", "rep"), "tensor", None),
        P(("group", "rep")),
        P("tensor", ("group", "rep")),
        P(("group", "rep"), "tensor"),
        P("tensor"),
        P(None, ("group", "tensor", "rep")),
        P(),
        P(),
        P(),
    )
    return jax.shard_map(
        shards,
        mesh=mesh,
        in_specs=placed,
        out_specs=(P(("group", "rep"), "tensor"), P(), P()),
        check_vma=False,
    )
```

```python
import functools
import math

import jax
import jax.numpy as jnp
from jax import lax
from jax.experimental import pallas as pl
from jax.experimental.pallas import tpu as pltpu
from jax.sharding import PartitionSpec as P

cut_slope = 4.0
MESH = pl.DeviceIdType.MESH


axes = ("group", "tensor", "rep")


def local_wait(ref, sem):
    pltpu.make_async_copy(ref, ref, sem).wait()


def tail_kernel(
    sizes,
    probe_ref,
    keys_hbm,
    values_hbm,
    own_key_ref,
    own_value_ref,
    counts_ref,
    mixing_hbm,
    skip_ref,
    gain_ref,
    lexicon_hbm,
    sharp_ref,
    mu_ref,
    chosen_ref,
    hidden_ref,
    targets_ref,
    surprise_ref,
    keys,
    values,
    row_attn,
    attn_ref,
    mixing,
    lexicon,
    every_attn,
    part,
    incoming,
    skip_block,
    gains,
    square_sums,
    state,
    logits,
    stats,
    kept_parts,
    cache_sems,
    load_sems,
    attn_send,
    attn_recv,
    skip_send,
    skip_recv,
    gain_send,
    gain_recv,
    square_sems,
    part_send,
    part_recv,
    column_send,
    plane_send,
    pair_send,
    state_recv,
    stats_sems,
    kept_sems,
):
    G, T, R = sizes
    N = G * T * R
    columns = G * R
    fold = columns // T
    pairs = R // 2
    own_rows, heads, head_dim = probe_ref.shape
    kv_heads = own_key_ref.shape[1]
    cache_len = keys.shape[2]
    rows = every_attn.shape[0]
    block_rows = rows // T
    halves, half_rows = incoming.shape[1:3]
    width = mixing.shape[1]
    vocab_local = lexicon.shape[1]

    g, t, r = (lax.axis_index(a) for a in axes)
    pair, core = r // 2, r % 2
    other = 1 - core
    column = g * R + r
    twin = g * R + pair * 2 + other
    me = (g * T + t) * R + r

    load_mixing = pltpu.make_async_copy(mixing_hbm, mixing, load_sems.at[0])
    load_lexicon = pltpu.make_async_copy(lexicon_hbm, lexicon, load_sems.at[1])
    group_rows = own_rows // cache_sems.shape[1]

    def cache_loads(index):
        span = pl.ds(index * group_rows, group_rows)
        return [
            pltpu.make_async_copy(source.at[span], dest.at[span], cache_sems.at[n, index])
            for n, (source, dest) in enumerate(((keys_hbm, keys), (values_hbm, values)))
        ]

    @pl.loop(0, own_rows // group_rows)
    def _(index):
        for load in cache_loads(index):
            load.start()

    load_mixing.start()

    def wrap(position, size):
        return jnp.where(position >= size, position - size, position)

    def every_other(visit):
        for a in range(G):
            to_g = wrap(g + a, G)

            @pl.loop(1 if a == 0 else 0, T)
            def _(b):
                to_t = wrap(t + b, T)
                for d in range(R):
                    visit((to_g, to_t, wrap(r + d, R)))

        for d in range(1, R):
            visit((g, t, wrap(r + d, R)))

    barrier = pltpu.get_barrier_semaphore()
    every_other(
        lambda device: pl.semaphore_signal(
            barrier, inc=1, device_id=device, device_id_type=MESH
        )
    )

    score_scale = 1.0 / math.sqrt(head_dim)
    share_of = heads // kv_heads
    position = lax.broadcasted_iota(jnp.int32, (heads, cache_len), 1)

    def spread_heads(pair_rows):
        wide = pair_rows.astype(jnp.float32)
        return jnp.concatenate(
            [jnp.broadcast_to(wide[k : k + 1], (share_of, head_dim)) for k in range(kv_heads)],
            axis=0,
        )

    def per_head(products):
        return jnp.concatenate(
            [products[k][k * share_of : (k + 1) * share_of] for k in range(kv_heads)], axis=0
        )

    def attend(row):
        query = probe_ref[row]
        scores = score_scale * per_head(
            [
                lax.dot_general(
                    query,
                    keys[row, k],
                    (((1,), (1,)), ((), ())),
                    preferred_element_type=jnp.float32,
                )
                for k in range(kv_heads)
            ]
        )
        own = score_scale * jnp.sum(
            query.astype(jnp.float32) * spread_heads(own_key_ref[row]), axis=1, keepdims=True
        )
        live = position < counts_ref[row]
        peak = jnp.maximum(
            jnp.max(jnp.where(live, scores, -1e30), axis=1, keepdims=True), own
        )
        expo = jnp.where(live, jnp.exp(scores - peak), 0.0)
        own_expo = jnp.exp(own - peak)
        total = jnp.sum(expo, axis=1, keepdims=True) + own_expo
        weights = expo.astype(jnp.bfloat16)
        accum = per_head(
            [
                jnp.dot(weights, values[row, k], preferred_element_type=jnp.float32)
                for k in range(kv_heads)
            ]
        )
        own_weight = own_expo.astype(jnp.bfloat16).astype(jnp.float32)
        accum = accum + own_weight * spread_heads(own_value_ref[row])
        row_attn[row] = accum / total

    @pl.loop(0, own_rows // group_rows)
    def _(index):
        for load in cache_loads(index):
            load.wait()
        for n in range(group_rows):
            attend(index * group_rows + n)

    for h in range(heads):
        attn_ref[:, h * head_dim : (h + 1) * head_dim] = row_attn[:, h, :].astype(jnp.bfloat16)

    load_lexicon.start()
    pl.semaphore_wait(barrier, N - 1)

    def push(src, dst, send_sem, recv_sem, device):
        copy = pltpu.make_async_remote_copy(
            src_ref=src,
            dst_ref=dst,
            send_sem=send_sem,
            recv_sem=recv_sem,
            device_id=device,
            device_id_type=MESH,
        )
        copy.start()
        return copy

    peers = [(a, b) for a in range(G) for b in range(pairs) if (a, b) != (0, 0)]

    def peer_to(a, b):
        return (g + a) % G, ((pair + b) % pairs) * 2 + core

    def peer_from(a, b):
        return ((g + G - a) % G) * R + ((pair + pairs - b) % pairs) * 2

    sibling = (g, t, pair * 2 + other)

    def attn_rows(index):
        return every_attn.at[pl.ds(pl.multiple_of(index * own_rows, own_rows), own_rows), :]

    sends = []
    for n, (a, b) in enumerate(peers):
        to_g, to_r = peer_to(a, b)
        sends.append(
            push(attn_ref, attn_rows(column), attn_send.at[n], attn_recv.at[column], (to_g, t, to_r))
        )
    sends.append(
        push(attn_ref, attn_rows(column), attn_send.at[len(peers)], attn_recv.at[column], sibling)
    )
    every_attn[pl.ds(pl.multiple_of(column * own_rows, own_rows), own_rows), :] = attn_ref[...]

    home_t = column // fold
    home_slot = column % fold

    def skip_rows(slot):
        return skip_block.at[pl.ds(pl.multiple_of(slot * own_rows, own_rows), own_rows), :]

    for j in range(fold):
        dest = t * fold + j
        away = jnp.logical_or(dest != column, home_t != t)
        source = skip_ref.at[:, pl.ds(j * width, width)]

        @pl.when(away)
        def _():
            push(
                source,
                skip_rows(home_slot),
                skip_send.at[j],
                skip_recv.at[home_slot],
                (dest // R, home_t, dest % R),
            )

        @pl.when(jnp.logical_not(away))
        def _():
            pltpu.make_async_copy(source, skip_rows(home_slot), skip_recv.at[home_slot]).start()

    gains[pl.ds(t * fold, fold)] = gain_ref[...]
    for j in range(1, T):
        sends.append(
            push(
                gain_ref,
                gains.at[pl.ds(t * fold, fold)],
                gain_send.at[j],
                gain_recv.at[t],
                (g, (t + j) % T, r),
            )
        )

    for n, (a, b) in enumerate(peers):
        source = peer_from(a, b) + core
        local_wait(attn_rows(source), attn_recv.at[source])
        sends.append(
            push(
                attn_rows(source),
                attn_rows(source),
                attn_send.at[len(peers) + 1 + n],
                attn_recv.at[source],
                sibling,
            )
        )
    local_wait(attn_rows(twin), attn_recv.at[twin])
    for a, b in peers:
        source = peer_from(a, b) + other
        local_wait(attn_rows(source), attn_recv.at[source])

    load_mixing.wait()
    tile = min(256, width)

    @pl.loop(0, width // tile)
    def _(index):
        span = pl.ds(pl.multiple_of(index * tile, tile), tile)
        part[:, span] = jnp.dot(
            every_attn[...], mixing[:, span], preferred_element_type=jnp.float32
        )

    def block_of(index, half):
        start = pl.multiple_of((index * halves + half) * half_rows, half_rows)
        return pl.ds(start, half_rows)

    for half in range(halves):
        for j in range(1, T):
            to_t = (t + j) % T
            sends.append(
                push(
                    part.at[block_of(to_t, half), :],
                    incoming.at[t, half],
                    part_send.at[j, half],
                    part_recv.at[t, half],
                    (g, to_t, r),
                )
            )
    for j in range(fold):
        local_wait(skip_rows(j), skip_recv.at[j])

    def state_block(col, index, half):
        return state.at[col, block_of(index, half), :]

    def spread(index, half):
        block = state_block(column, index, half)
        for a, b in peers:
            to_g, to_r = peer_to(a, b)
            push(block, block, plane_send, state_recv.at[column, index, half], (to_g, t, to_r))
        push(block, block, plane_send, state_recv.at[column, index, half], sibling)

    for half in range(halves):
        total = part[block_of(t, half), :]
        for j in range(1, T):
            from_t = (t + j) % T
            local_wait(incoming.at[from_t, half], part_recv.at[from_t, half])
            total = total + incoming[from_t, half]
        residual = skip_block[half * half_rows : (half + 1) * half_rows, :].astype(jnp.float32)
        state[column, block_of(t, half), :] = (residual + total).astype(jnp.bfloat16)
        block = state_block(column, t, half)
        for j in range(1, T):
            push(
                block,
                block,
                column_send,
                state_recv.at[column, t, half],
                (g, (t + j) % T, r),
            )
        spread(t, half)

    def arrive(col):
        for half in range(halves):
            for j in range(T):
                from_t = (t + j) % T
                local_wait(state_block(col, from_t, half), state_recv.at[col, from_t, half])

    for half in range(halves):
        for j in range(1, T):
            from_t = (t + j) % T
            local_wait(
                state_block(column, from_t, half), state_recv.at[column, from_t, half]
            )
            spread(from_t, half)

    wide = state[column].astype(jnp.float32)
    row_squares = jnp.sum(wide * wide, axis=1, keepdims=True)
    diagonal = lax.broadcasted_iota(jnp.int32, (rows, rows), 1) == (
        lax.broadcasted_iota(jnp.int32, (rows, rows), 0)
    )
    square_sums[column] = jnp.sum(
        jnp.where(diagonal, row_squares, 0.0), axis=0, keepdims=True
    )
    for a in range(G):
        for d in range(R):
            if (a, d) != (0, 0):
                push(
                    square_sums.at[column],
                    square_sums.at[column],
                    square_sems.at[0],
                    square_sems.at[1],
                    (wrap(g + a, G), t, wrap(r + d, R)),
                )
    for j in range(1, T):
        from_t = (t + j) % T
        local_wait(gains.at[pl.ds(from_t * fold, fold)], gain_recv.at[from_t])
    load_lexicon.wait()
    local_wait(square_sums.at[pl.ds(0, columns - 1)], square_sems.at[1])
    mean_square = jnp.sum(square_sums[...], axis=0) / (columns * width)
    scale = lax.rsqrt(
        jnp.sum(jnp.where(diagonal, mean_square, 0.0), axis=1, keepdims=True) + 1e-05
    )
    logits[...] = jnp.zeros_like(logits)

    def head(col):
        normed = (state[col].astype(jnp.float32) * scale * gains[col]).astype(jnp.bfloat16)
        block = lexicon[pl.ds(pl.multiple_of(col * width, width), width), :]
        logits[...] += jnp.dot(normed, block, preferred_element_type=jnp.float32)

    head(column)
    arrive(twin)
    head(twin)

    @pl.loop(1, G * pairs)
    def _(step):
        source = peer_from(step // pairs, step % pairs)
        for half in range(halves):
            for j in range(T):
                from_t = (t + j) % T
                block = state_block(source + core, from_t, half)
                sem = state_recv.at[source + core, from_t, half]
                local_wait(block, sem)
                push(block, block, pair_send, sem, sibling)
        head(source + core)
        arrive(source + other)
        head(source + other)

    own_span = pl.ds(pl.multiple_of(column * own_rows, own_rows), own_rows)
    for j in range(fold):
        hidden_ref[:, j * width : (j + 1) * width] = state[t * fold + j, own_span, :]

    odds = logits[...].T * sharp_ref[...]
    entry = me * vocab_local + lax.broadcasted_iota(jnp.int32, odds.shape, 0)
    token_part = jnp.sum(jnp.where(entry == chosen_ref[...], odds, 0.0), axis=0, keepdims=True)
    local_top = jnp.max(odds, axis=0, keepdims=True)
    local_total = jnp.sum(jnp.exp(odds - local_top), axis=0, keepdims=True)
    stats[me] = jnp.concatenate(
        [local_top, local_total, token_part, jnp.zeros((5, rows), jnp.float32)], axis=0
    )

    def share(buffer, sems):
        every_other(
            lambda device: push(
                buffer.at[me], buffer.at[me], sems.at[0], sems.at[1], device
            )
        )
        local_wait(buffer.at[pl.ds(0, N - 1)], sems.at[1])

    share(stats, stats_sems)
    tops = stats[:, 0, :]
    top = jnp.max(tops, axis=0, keepdims=True)
    sum_exp = jnp.sum(stats[:, 1, :] * jnp.exp(tops - top), axis=0, keepdims=True)
    token_logit = jnp.sum(stats[:, 2, :], axis=0, keepdims=True)
    lognorm = top + jnp.log(sum_exp)
    mu = mu_ref[...]
    logp = odds - lognorm
    margin = cut_slope * (mu + logp / math.log(2.0))
    tail = jnp.exp(-jnp.abs(margin))
    weight = jnp.where(margin >= 0.0, 1.0, tail) / (1.0 + tail)
    kept_local = jnp.sum(jnp.exp(logp) * weight, axis=0, keepdims=True)
    kept_parts[me] = kept_local
    share(kept_parts, kept_sems)
    kept = jnp.sum(kept_parts[...], axis=0)
    token_logp = token_logit - lognorm
    token_margin = cut_slope * (mu + token_logp / math.log(2.0))
    token_logw = (
        token_logp
        + jnp.minimum(token_margin, 0.0)
        - jnp.log1p(jnp.exp(-jnp.abs(token_margin)))
    )
    surprise = -(token_logw - jnp.log(kept)) / math.log(2.0)
    surprise_ref[...] = surprise
    targets_ref[...] = mu - 0.1 * (surprise - 5.0)

    for copy in sends:
        copy.wait_send()
    for j in range(fold):
        away = jnp.logical_or(t * fold + j != column, home_t != t)

        @pl.when(away)
        def _():
            local_wait(skip_ref.at[:, pl.ds(j * width, width)], skip_send.at[j])

    local_wait(square_sums.at[pl.ds(0, columns - 1)], square_sems.at[0])
    local_wait(state.at[0, pl.ds(0, (T - 1) * block_rows), :], column_send)
    local_wait(state.at[pl.ds(0, len(peers) + 1)], plane_send)
    local_wait(state.at[pl.ds(0, len(peers))], pair_send)
    local_wait(stats.at[pl.ds(0, N - 1)], stats_sems.at[0])
    local_wait(kept_parts.at[pl.ds(0, N - 1)], kept_sems.at[0])


def finish_kernel(hidden_in, targets_in, surprise_in, hidden_ref, targets_ref, surprise_ref):
    hidden_ref[...] = hidden_in[...]
    targets_ref[...] = targets_in[...]
    surprise_ref[...] = surprise_in[...]


def tail(sizes, probe, keys, values, own_key, own_value, counts, mixing, skip, gain, lexicon, sharp, mu, chosen):
    G, T, R = sizes
    N = G * T * R
    columns = G * R
    fold = columns // T
    own_rows, heads, head_dim = probe.shape
    load_groups = math.gcd(own_rows, 4)
    rows = own_rows * columns
    block_rows = rows // T
    width = mixing.shape[1]
    depth = mixing.shape[0]
    features, vocab_local = lexicon.shape
    peers = columns // 2 - 1
    halves = 2
    vmem = pl.BlockSpec(memory_space=pltpu.VMEM)
    hbm = pl.BlockSpec(memory_space=pl.ANY)
    dma = pltpu.SemaphoreType.DMA
    out_shape = (
        jax.ShapeDtypeStruct(skip.shape, jnp.bfloat16),
        jax.ShapeDtypeStruct((1, rows), jnp.float32),
        jax.ShapeDtypeStruct((1, rows), jnp.float32),
    )
    results = pl.pallas_call(
        functools.partial(tail_kernel, sizes),
        out_shape=out_shape,
        in_specs=[vmem, hbm, hbm, vmem, vmem, pl.BlockSpec(memory_space=pltpu.SMEM), hbm, vmem, vmem, hbm, vmem, vmem, vmem],
        out_specs=(vmem, vmem, vmem),
        scratch_shapes=[
            pltpu.VMEM(keys.shape, jnp.bfloat16),
            pltpu.VMEM(values.shape, jnp.bfloat16),
            pltpu.VMEM((own_rows, heads, head_dim), jnp.float32),
            pltpu.VMEM((own_rows, depth), jnp.bfloat16),
            pltpu.VMEM(mixing.shape, jnp.bfloat16),
            pltpu.VMEM(lexicon.shape, jnp.bfloat16),
            pltpu.VMEM((rows, depth), jnp.bfloat16),
            pltpu.VMEM((rows, width), jnp.float32),
            pltpu.VMEM((T, halves, block_rows // halves, width), jnp.float32),
            pltpu.VMEM((block_rows, width), jnp.bfloat16),
            pltpu.VMEM((columns, 1, width), jnp.float32),
            pltpu.VMEM((columns, 1, rows), jnp.float32),
            pltpu.VMEM((columns, rows, width), jnp.bfloat16),
            pltpu.VMEM((rows, vocab_local), jnp.float32),
            pltpu.VMEM((N, 8, rows), jnp.float32),
            pltpu.VMEM((N, 1, rows), jnp.float32),
            dma((2, load_groups)),
            dma((2,)),
            dma((2 * peers + 1,)),
            dma((columns,)),
            dma((fold,)),
            dma((fold,)),
            dma((T,)),
            dma((T,)),
            dma((2,)),
            dma((T, halves)),
            dma((T, halves)),
            dma,
            dma,
            dma,
            dma((columns, T, halves)),
            dma((2,)),
            dma((2,)),
        ],
        compiler_params=pltpu.CompilerParams(
            collective_id=0, has_side_effects=True, vmem_limit_bytes=56 * 2**20
        ),
    )(
        probe,
        keys,
        values,
        own_key,
        own_value,
        counts,
        mixing,
        skip,
        gain.astype(jnp.float32).reshape(fold, 1, width),
        lexicon,
        sharp.reshape(1, rows),
        mu.reshape(1, rows),
        chosen.reshape(1, rows),
    )
    hidden, targets, surprise = pl.pallas_call(
        finish_kernel, out_shape=out_shape, in_specs=[vmem] * 3, out_specs=(vmem,) * 3
    )(*results)
    return hidden, targets.reshape(rows), surprise.reshape(rows)


def solution(mesh):
    sizes = tuple(mesh.shape[a] for a in axes)

    def shards(
        probe_vectors,
        stored_lookup_vectors,
        stored_content_vectors,
        fresh_lookup_vector,
        fresh_content_vector,
        history_counts,
        mixing_matrix,
        skip_stream,
        closing_multiplier,
        lexicon_matrix,
        sharpening_factor,
        desired_perplexity,
        chosen_symbols,
    ):
        return tail(
            sizes,
            probe_vectors,
            stored_lookup_vectors,
            stored_content_vectors,
            fresh_lookup_vector,
            fresh_content_vector,
            history_counts,
            mixing_matrix,
            skip_stream,
            closing_multiplier,
            lexicon_matrix,
            sharpening_factor,
            desired_perplexity,
            chosen_symbols,
        )

    placed = (
        P(("group", "rep"), "tensor", None),
        P(("group", "rep"), "tensor", None, None),
        P(("group", "rep"), "tensor", None, None),
        P(("group", "rep"), "tensor", None),
        P(("group", "rep"), "tensor", None),
        P(("group", "rep")),
        P("tensor", ("group", "rep")),
        P(("group", "rep"), "tensor"),
        P("tensor"),
        P(None, ("group", "tensor", "rep")),
        P(),
        P(),
        P(),
    )
    return jax.shard_map(
        shards,
        mesh=mesh,
        in_specs=placed,
        out_specs=(P(("group", "rep"), "tensor"), P(), P()),
        check_vma=False,
    )
```

```python
import functools
import math

import jax
import jax.numpy as jnp
from jax import lax
from jax.experimental import pallas as pl
from jax.experimental.pallas import tpu as pltpu
from jax.sharding import PartitionSpec as P

cut_slope = 4.0
MESH = pl.DeviceIdType.MESH


axes = ("group", "tensor", "rep")


def local_wait(ref, sem):
    pltpu.make_async_copy(ref, ref, sem).wait()


def tail_kernel(
    sizes,
    probe_ref,
    keys_hbm,
    values_hbm,
    own_key_ref,
    own_value_ref,
    counts_ref,
    mixing_hbm,
    skip_ref,
    gain_ref,
    lexicon_hbm,
    sharp_ref,
    mu_ref,
    chosen_ref,
    hidden_ref,
    targets_ref,
    surprise_ref,
    keys,
    values,
    row_attn,
    attn_ref,
    mixing,
    lexicon,
    every_attn,
    part,
    incoming,
    skip_block,
    gains,
    square_sums,
    state,
    logits,
    column_stats,
    plane_stats,
    column_kept,
    plane_kept,
    cache_sems,
    load_sems,
    attn_send,
    attn_recv,
    skip_send,
    skip_recv,
    gain_send,
    gain_recv,
    square_sems,
    part_send,
    part_recv,
    column_send,
    plane_send,
    pair_send,
    state_recv,
    stats_sems,
    kept_sems,
):
    G, T, R = sizes
    columns = G * R
    fold = columns // T
    pairs = R // 2
    own_rows, heads, head_dim = probe_ref.shape
    kv_heads = own_key_ref.shape[1]
    cache_len = keys.shape[2]
    rows = every_attn.shape[0]
    block_rows = rows // T
    halves, half_rows = incoming.shape[1:3]
    width = mixing.shape[1]
    vocab_local = lexicon.shape[1]

    g, t, r = (lax.axis_index(a) for a in axes)
    pair, core = r // 2, r % 2
    other = 1 - core
    column = g * R + r
    twin = g * R + pair * 2 + other
    me = (g * T + t) * R + r

    load_mixing = pltpu.make_async_copy(mixing_hbm, mixing, load_sems.at[0])
    load_lexicon = pltpu.make_async_copy(lexicon_hbm, lexicon, load_sems.at[1])
    group_rows = own_rows // cache_sems.shape[1]

    def cache_loads(index):
        span = pl.ds(index * group_rows, group_rows)
        return [
            pltpu.make_async_copy(source.at[span], dest.at[span], cache_sems.at[n, index])
            for n, (source, dest) in enumerate(((keys_hbm, keys), (values_hbm, values)))
        ]

    @pl.loop(0, own_rows // group_rows)
    def _(index):
        for load in cache_loads(index):
            load.start()

    load_mixing.start()

    def wrap(position, size):
        return jnp.where(position >= size, position - size, position)

    partners = [(g, wrap(t + b, T), r) for b in range(1, T)]
    partners += [
        (wrap(g + a, G), t, wrap(r + d, R)) for a in range(G) for d in range(R) if (a, d) != (0, 0)
    ]
    barrier = pltpu.get_barrier_semaphore()
    for device in partners:
        pl.semaphore_signal(barrier, inc=1, device_id=device, device_id_type=MESH)

    home_t = column // fold
    home_slot = column % fold
    homes = []
    for j in range(fold):
        dest = t * fold + j
        away = jnp.logical_or(dest != column, home_t != t)
        homes.append((away, (dest // R, home_t, dest % R)))

        @pl.when(away)
        def _():
            pl.semaphore_signal(
                barrier, inc=1, device_id=homes[j][1], device_id_type=MESH
            )

    score_scale = 1.0 / math.sqrt(head_dim)
    share_of = heads // kv_heads
    position = lax.broadcasted_iota(jnp.int32, (heads, cache_len), 1)

    def spread_heads(pair_rows):
        wide = pair_rows.astype(jnp.float32)
        return jnp.concatenate(
            [jnp.broadcast_to(wide[k : k + 1], (share_of, head_dim)) for k in range(kv_heads)],
            axis=0,
        )

    def per_head(products):
        return jnp.concatenate(
            [products[k][k * share_of : (k + 1) * share_of] for k in range(kv_heads)], axis=0
        )

    def attend(row):
        query = probe_ref[row]
        scores = score_scale * per_head(
            [
                lax.dot_general(
                    query,
                    keys[row, k],
                    (((1,), (1,)), ((), ())),
                    preferred_element_type=jnp.float32,
                )
                for k in range(kv_heads)
            ]
        )
        own = score_scale * jnp.sum(
            query.astype(jnp.float32) * spread_heads(own_key_ref[row]), axis=1, keepdims=True
        )
        live = position < counts_ref[row]
        peak = jnp.maximum(
            jnp.max(jnp.where(live, scores, -1e30), axis=1, keepdims=True), own
        )
        expo = jnp.where(live, jnp.exp(scores - peak), 0.0)
        own_expo = jnp.exp(own - peak)
        total = jnp.sum(expo, axis=1, keepdims=True) + own_expo
        weights = expo.astype(jnp.bfloat16)
        accum = per_head(
            [
                jnp.dot(weights, values[row, k], preferred_element_type=jnp.float32)
                for k in range(kv_heads)
            ]
        )
        own_weight = own_expo.astype(jnp.bfloat16).astype(jnp.float32)
        accum = accum + own_weight * spread_heads(own_value_ref[row])
        row_attn[row] = accum / total

    @pl.loop(0, own_rows // group_rows)
    def _(index):
        for load in cache_loads(index):
            load.wait()
        for n in range(group_rows):
            attend(index * group_rows + n)

    for h in range(heads):
        attn_ref[:, h * head_dim : (h + 1) * head_dim] = row_attn[:, h, :].astype(jnp.bfloat16)

    load_lexicon.start()
    pl.semaphore_wait(
        barrier, len(partners) + sum(jnp.where(away, 1, 0) for away, _ in homes)
    )


    def push(src, dst, send_sem, recv_sem, device):
        copy = pltpu.make_async_remote_copy(
            src_ref=src,
            dst_ref=dst,
            send_sem=send_sem,
            recv_sem=recv_sem,
            device_id=device,
            device_id_type=MESH,
        )
        copy.start()
        return copy

    peers = [(a, b) for a in range(G) for b in range(pairs) if (a, b) != (0, 0)]

    def peer_to(a, b):
        return (g + a) % G, ((pair + b) % pairs) * 2 + core

    def peer_from(a, b):
        return ((g + G - a) % G) * R + ((pair + pairs - b) % pairs) * 2

    sibling = (g, t, pair * 2 + other)

    def attn_rows(index):
        return every_attn.at[pl.ds(pl.multiple_of(index * own_rows, own_rows), own_rows), :]

    sends = []
    for n, (a, b) in enumerate(peers):
        to_g, to_r = peer_to(a, b)
        sends.append(
            push(attn_ref, attn_rows(column), attn_send.at[n], attn_recv.at[column], (to_g, t, to_r))
        )
    sends.append(
        push(attn_ref, attn_rows(column), attn_send.at[len(peers)], attn_recv.at[column], sibling)
    )
    every_attn[pl.ds(pl.multiple_of(column * own_rows, own_rows), own_rows), :] = attn_ref[...]

    def skip_rows(slot):
        return skip_block.at[pl.ds(pl.multiple_of(slot * own_rows, own_rows), own_rows), :]

    for j in range(fold):
        away, home = homes[j]
        source = skip_ref.at[:, pl.ds(j * width, width)]

        @pl.when(away)
        def _():
            push(
                source,
                skip_rows(home_slot),
                skip_send.at[j],
                skip_recv.at[home_slot],
                home,
            )

        @pl.when(jnp.logical_not(away))
        def _():
            pltpu.make_async_copy(source, skip_rows(home_slot), skip_recv.at[home_slot]).start()

    gains[pl.ds(t * fold, fold)] = gain_ref[...]
    for j in range(1, T):
        sends.append(
            push(
                gain_ref,
                gains.at[pl.ds(t * fold, fold)],
                gain_send.at[j],
                gain_recv.at[t],
                (g, (t + j) % T, r),
            )
        )

    for n, (a, b) in enumerate(peers):
        source = peer_from(a, b) + core
        local_wait(attn_rows(source), attn_recv.at[source])
        sends.append(
            push(
                attn_rows(source),
                attn_rows(source),
                attn_send.at[len(peers) + 1 + n],
                attn_recv.at[source],
                sibling,
            )
        )
    local_wait(attn_rows(twin), attn_recv.at[twin])
    for a, b in peers:
        source = peer_from(a, b) + other
        local_wait(attn_rows(source), attn_recv.at[source])

    load_mixing.wait()
    tile = min(256, width)

    @pl.loop(0, width // tile)
    def _(index):
        span = pl.ds(pl.multiple_of(index * tile, tile), tile)
        part[:, span] = jnp.dot(
            every_attn[...], mixing[:, span], preferred_element_type=jnp.float32
        )

    def block_of(index, half):
        start = pl.multiple_of((index * halves + half) * half_rows, half_rows)
        return pl.ds(start, half_rows)

    for half in range(halves):
        for j in range(1, T):
            to_t = (t + j) % T
            sends.append(
                push(
                    part.at[block_of(to_t, half), :],
                    incoming.at[t, half],
                    part_send.at[j, half],
                    part_recv.at[t, half],
                    (g, to_t, r),
                )
            )
    for j in range(fold):
        local_wait(skip_rows(j), skip_recv.at[j])

    def state_block(col, index, half):
        return state.at[col, block_of(index, half), :]

    def spread(index, half):
        block = state_block(column, index, half)
        for a, b in peers:
            to_g, to_r = peer_to(a, b)
            push(block, block, plane_send, state_recv.at[column, index, half], (to_g, t, to_r))
        push(block, block, plane_send, state_recv.at[column, index, half], sibling)

    for half in range(halves):
        total = part[block_of(t, half), :]
        for j in range(1, T):
            from_t = (t + j) % T
            local_wait(incoming.at[from_t, half], part_recv.at[from_t, half])
            total = total + incoming[from_t, half]
        residual = skip_block[half * half_rows : (half + 1) * half_rows, :].astype(jnp.float32)
        state[column, block_of(t, half), :] = (residual + total).astype(jnp.bfloat16)
        block = state_block(column, t, half)
        for j in range(1, T):
            push(
                block,
                block,
                column_send,
                state_recv.at[column, t, half],
                (g, (t + j) % T, r),
            )
        spread(t, half)

    def arrive(col):
        for half in range(halves):
            for j in range(T):
                from_t = (t + j) % T
                local_wait(state_block(col, from_t, half), state_recv.at[col, from_t, half])

    for half in range(halves):
        for j in range(1, T):
            from_t = (t + j) % T
            local_wait(
                state_block(column, from_t, half), state_recv.at[column, from_t, half]
            )
            spread(from_t, half)

    wide = state[column].astype(jnp.float32)
    row_squares = jnp.sum(wide * wide, axis=1, keepdims=True)
    diagonal = lax.broadcasted_iota(jnp.int32, (rows, rows), 1) == (
        lax.broadcasted_iota(jnp.int32, (rows, rows), 0)
    )
    square_sums[column] = jnp.sum(
        jnp.where(diagonal, row_squares, 0.0), axis=0, keepdims=True
    )
    for a in range(G):
        for d in range(R):
            if (a, d) != (0, 0):
                push(
                    square_sums.at[column],
                    square_sums.at[column],
                    square_sems.at[0],
                    square_sems.at[1],
                    (wrap(g + a, G), t, wrap(r + d, R)),
                )
    for j in range(1, T):
        from_t = (t + j) % T
        local_wait(gains.at[pl.ds(from_t * fold, fold)], gain_recv.at[from_t])
    load_lexicon.wait()
    local_wait(square_sums.at[pl.ds(0, columns - 1)], square_sems.at[1])
    mean_square = jnp.sum(square_sums[...], axis=0) / (columns * width)
    scale = lax.rsqrt(
        jnp.sum(jnp.where(diagonal, mean_square, 0.0), axis=1, keepdims=True) + 1e-05
    )
    logits[...] = jnp.zeros_like(logits)

    def head(col):
        normed = (state[col].astype(jnp.float32) * scale * gains[col]).astype(jnp.bfloat16)
        block = lexicon[pl.ds(pl.multiple_of(col * width, width), width), :]
        logits[...] += jnp.dot(normed, block, preferred_element_type=jnp.float32)

    head(column)
    arrive(twin)
    head(twin)

    @pl.loop(1, G * pairs)
    def _(step):
        source = peer_from(step // pairs, step % pairs)
        for half in range(halves):
            for j in range(T):
                from_t = (t + j) % T
                block = state_block(source + core, from_t, half)
                sem = state_recv.at[source + core, from_t, half]
                local_wait(block, sem)
                push(block, block, pair_send, sem, sibling)
        head(source + core)
        arrive(source + other)
        head(source + other)

    own_span = pl.ds(pl.multiple_of(column * own_rows, own_rows), own_rows)
    for j in range(fold):
        hidden_ref[:, j * width : (j + 1) * width] = state[t * fold + j, own_span, :]

    odds = logits[...].T * sharp_ref[...]
    entry = me * vocab_local + lax.broadcasted_iota(jnp.int32, odds.shape, 0)
    token_part = jnp.sum(jnp.where(entry == chosen_ref[...], odds, 0.0), axis=0, keepdims=True)
    local_top = jnp.max(odds, axis=0, keepdims=True)
    local_total = jnp.sum(jnp.exp(odds - local_top), axis=0, keepdims=True)
    spare = jnp.zeros((1, rows), jnp.float32)

    def share_column(buffer, sems):
        for j in range(1, T):
            push(buffer.at[t], buffer.at[t], sems.at[0], sems.at[1], (g, wrap(t + j, T), r))
        local_wait(buffer.at[pl.ds(0, T - 1)], sems.at[1])

    def share_plane(buffer, sems):
        for a in reversed(range(G)):
            for d in reversed(range(R)):
                if (a, d) != (0, 0):
                    push(
                        buffer.at[column],
                        buffer.at[column],
                        sems.at[0],
                        sems.at[1],
                        (wrap(g + a, G), t, wrap(r + d, R)),
                    )
        local_wait(buffer.at[pl.ds(0, columns - 1)], sems.at[1])

    def merge(buffer):
        tops = buffer[:, 0, :]
        top = jnp.max(tops, axis=0, keepdims=True)
        sum_exp = jnp.sum(buffer[:, 1, :] * jnp.exp(tops - top), axis=0, keepdims=True)
        return top, sum_exp, jnp.sum(buffer[:, 2, :], axis=0, keepdims=True)

    column_stats[t] = jnp.concatenate([local_top, local_total, token_part, spare], axis=0)
    share_column(column_stats, stats_sems.at[0])
    plane_stats[column] = jnp.concatenate([*merge(column_stats), spare], axis=0)
    share_plane(plane_stats, stats_sems.at[1])
    top, sum_exp, token_logit = merge(plane_stats)
    lognorm = top + jnp.log(sum_exp)
    mu = mu_ref[...]
    logp = odds - lognorm
    margin = cut_slope * (mu + logp / math.log(2.0))
    tail = jnp.exp(-jnp.abs(margin))
    weight = jnp.where(margin >= 0.0, 1.0, tail) / (1.0 + tail)
    kept_local = jnp.sum(jnp.exp(logp) * weight, axis=0, keepdims=True)
    column_kept[t] = kept_local
    share_column(column_kept, kept_sems.at[0])
    plane_kept[column] = jnp.sum(column_kept[...], axis=0)
    share_plane(plane_kept, kept_sems.at[1])
    kept = jnp.sum(plane_kept[...], axis=0)
    token_logp = token_logit - lognorm
    token_margin = cut_slope * (mu + token_logp / math.log(2.0))
    token_logw = (
        token_logp
        + jnp.minimum(token_margin, 0.0)
        - jnp.log1p(jnp.exp(-jnp.abs(token_margin)))
    )
    surprise = -(token_logw - jnp.log(kept)) / math.log(2.0)
    surprise_ref[...] = surprise
    targets_ref[...] = mu - 0.1 * (surprise - 5.0)

    for copy in sends:
        copy.wait_send()
    for j in range(fold):
        @pl.when(homes[j][0])
        def _():
            local_wait(skip_ref.at[:, pl.ds(j * width, width)], skip_send.at[j])

    local_wait(square_sums.at[pl.ds(0, columns - 1)], square_sems.at[0])
    local_wait(state.at[0, pl.ds(0, (T - 1) * block_rows), :], column_send)
    local_wait(state.at[pl.ds(0, len(peers) + 1)], plane_send)
    local_wait(state.at[pl.ds(0, len(peers))], pair_send)
    local_wait(column_stats.at[pl.ds(0, T - 1)], stats_sems.at[0, 0])
    local_wait(plane_stats.at[pl.ds(0, columns - 1)], stats_sems.at[1, 0])
    local_wait(column_kept.at[pl.ds(0, T - 1)], kept_sems.at[0, 0])
    local_wait(plane_kept.at[pl.ds(0, columns - 1)], kept_sems.at[1, 0])


def finish_kernel(hidden_in, targets_in, surprise_in, hidden_ref, targets_ref, surprise_ref):
    hidden_ref[...] = hidden_in[...]
    targets_ref[...] = targets_in[...]
    surprise_ref[...] = surprise_in[...]


def tail(sizes, probe, keys, values, own_key, own_value, counts, mixing, skip, gain, lexicon, sharp, mu, chosen):
    G, T, R = sizes
    columns = G * R
    fold = columns // T
    own_rows, heads, head_dim = probe.shape
    load_groups = math.gcd(own_rows, 4)
    rows = own_rows * columns
    block_rows = rows // T
    width = mixing.shape[1]
    depth = mixing.shape[0]
    features, vocab_local = lexicon.shape
    peers = columns // 2 - 1
    halves = 2
    vmem = pl.BlockSpec(memory_space=pltpu.VMEM)
    hbm = pl.BlockSpec(memory_space=pl.ANY)
    dma = pltpu.SemaphoreType.DMA
    out_shape = (
        jax.ShapeDtypeStruct(skip.shape, jnp.bfloat16),
        jax.ShapeDtypeStruct((1, rows), jnp.float32),
        jax.ShapeDtypeStruct((1, rows), jnp.float32),
    )
    results = pl.pallas_call(
        functools.partial(tail_kernel, sizes),
        out_shape=out_shape,
        in_specs=[vmem, hbm, hbm, vmem, vmem, pl.BlockSpec(memory_space=pltpu.SMEM), hbm, vmem, vmem, hbm, vmem, vmem, vmem],
        out_specs=(vmem, vmem, vmem),
        scratch_shapes=[
            pltpu.VMEM(keys.shape, jnp.bfloat16),
            pltpu.VMEM(values.shape, jnp.bfloat16),
            pltpu.VMEM((own_rows, heads, head_dim), jnp.float32),
            pltpu.VMEM((own_rows, depth), jnp.bfloat16),
            pltpu.VMEM(mixing.shape, jnp.bfloat16),
            pltpu.VMEM(lexicon.shape, jnp.bfloat16),
            pltpu.VMEM((rows, depth), jnp.bfloat16),
            pltpu.VMEM((rows, width), jnp.float32),
            pltpu.VMEM((T, halves, block_rows // halves, width), jnp.float32),
            pltpu.VMEM((block_rows, width), jnp.bfloat16),
            pltpu.VMEM((columns, 1, width), jnp.float32),
            pltpu.VMEM((columns, 1, rows), jnp.float32),
            pltpu.VMEM((columns, rows, width), jnp.bfloat16),
            pltpu.VMEM((rows, vocab_local), jnp.float32),
            pltpu.VMEM((T, 4, rows), jnp.float32),
            pltpu.VMEM((columns, 4, rows), jnp.float32),
            pltpu.VMEM((T, 1, rows), jnp.float32),
            pltpu.VMEM((columns, 1, rows), jnp.float32),
            dma((2, load_groups)),
            dma((2,)),
            dma((2 * peers + 1,)),
            dma((columns,)),
            dma((fold,)),
            dma((fold,)),
            dma((T,)),
            dma((T,)),
            dma((2,)),
            dma((T, halves)),
            dma((T, halves)),
            dma,
            dma,
            dma,
            dma((columns, T, halves)),
            dma((2, 2)),
            dma((2, 2)),
        ],
        compiler_params=pltpu.CompilerParams(
            collective_id=0, has_side_effects=True, vmem_limit_bytes=56 * 2**20
        ),
    )(
        probe,
        keys,
        values,
        own_key,
        own_value,
        counts,
        mixing,
        skip,
        gain.astype(jnp.float32).reshape(fold, 1, width),
        lexicon,
        sharp.reshape(1, rows),
        mu.reshape(1, rows),
        chosen.reshape(1, rows),
    )
    hidden, targets, surprise = pl.pallas_call(
        finish_kernel, out_shape=out_shape, in_specs=[vmem] * 3, out_specs=(vmem,) * 3
    )(*results)
    return hidden, targets.reshape(rows), surprise.reshape(rows)


def solution(mesh):
    sizes = tuple(mesh.shape[a] for a in axes)

    def shards(
        probe_vectors,
        stored_lookup_vectors,
        stored_content_vectors,
        fresh_lookup_vector,
        fresh_content_vector,
        history_counts,
        mixing_matrix,
        skip_stream,
        closing_multiplier,
        lexicon_matrix,
        sharpening_factor,
        desired_perplexity,
        chosen_symbols,
    ):
        return tail(
            sizes,
            probe_vectors,
            stored_lookup_vectors,
            stored_content_vectors,
            fresh_lookup_vector,
            fresh_content_vector,
            history_counts,
            mixing_matrix,
            skip_stream,
            closing_multiplier,
            lexicon_matrix,
            sharpening_factor,
            desired_perplexity,
            chosen_symbols,
        )

    placed = (
        P(("group", "rep"), "tensor", None),
        P(("group", "rep"), "tensor", None, None),
        P(("group", "rep"), "tensor", None, None),
        P(("group", "rep"), "tensor", None),
        P(("group", "rep"), "tensor", None),
        P(("group", "rep")),
        P("tensor", ("group", "rep")),
        P(("group", "rep"), "tensor"),
        P("tensor"),
        P(None, ("group", "tensor", "rep")),
        P(),
        P(),
        P(),
    )
    return jax.shard_map(
        shards,
        mesh=mesh,
        in_specs=placed,
        out_specs=(P(("group", "rep"), "tensor"), P(), P()),
        check_vma=False,
    )
```
